128 devices in a mesh: ctx: 16 (over x, y), tp: 8 (over z, core).
Axes of the slice: x: 4, y: 4, z: 4, core: 2. Of those that a mesh axis runs over, the one named last changes fastest.
Arguments:
- tokens: bfloat16 [4096, 8192], P(('ctx', 'tp')), may hold values from -6 to 6
- in_weight: bfloat16 [8192, 3, 4096], P(None, None, 'tp'), may hold values from -0.0625 to 0.0625
- short_filter: float32 [3, 3, 4096], P(None, None, 'tp'), may hold values from -3 to 3
- mr_filter: float32 [128, 256], P(None, 'tp'), may hold values from -0.35355338 to 0.35355338
- mr_bias: float32 [4096], P('tp'), may hold values from -4 to 4
- out_weight: bfloat16 [4096, 8192], P('tp', 'ctx'), may hold values from -0.09375 to 0.09375
Outputs:
- mixed: bfloat16 [4096, 8192], P(('ctx', 'tp'))
The draws below stay inside these ranges and needn't reach their ends.
All inputs are finite; a program needn't handle non-finite values.
Results may differ from the reference program's by a relative error of at most 0.018.
Values may be sent and summed in bfloat16 or wider, within the bound.
No kernel may reach another device: no remote copies, remote signals or barrier semaphores. Data moves between devices by JAX's collectives and lax.ppermute only.
A program may use at most 192 MiB of HBM per device.

```python
import jax
import jax.numpy as jnp
from jax import lax

D = 8192
H = 4096
GS = 16
KM = 128
G = 256
TOKENS = 4096
N_TP = 8


def steps_of(own_key, shape, shards, least, largest):
    loudness = 1.0
    for position, parts in shards:
        draws = jax.random.uniform(jax.random.fold_in(jax.random.fold_in(own_key, 6), position), (parts,), jnp.float32, least / len(shards), largest / len(shards))
        loudness = loudness * jnp.repeat(jnp.exp(draws), shape[position] // parts).reshape((-1,) + (1,) * (len(shape) - 1 - position))
    return loudness


def centred(rng, shape, spread, bound, cuts=(), held_as=jnp.bfloat16):
    entries = jax.random.normal(rng, shape, jnp.float32) * spread
    if len(cuts) > 0:
        entries = steps_of(rng, shape, cuts, -0.22, 0.18) * entries
    return jnp.clip(entries, min=-bound, max=bound).astype(held_as)


def setup_inputs(seed: int = 0) -> dict:
    streams_of = jax.random.split(jax.random.key(seed), 7)
    tokens = centred(streams_of[0], (TOKENS, D), 1.0, 6.0, ((0, 128),))
    in_weight = centred(streams_of[1], (D, 3, H), D ** -0.5, 0.0625, ((2, 8),))
    short_filter = centred(streams_of[2], (3, 3, H), 0.6, 3.0, ((2, 8),), jnp.float32)
    mr_filter = centred(streams_of[3], (KM, G), (1.0 / KM ** 0.5), 0.35355338, ((1, 8),), jnp.float32)
    mr_bias = centred(streams_of[4], (H,), 1.0, 4.0, ((0, 8),), jnp.float32)
    out_weight = centred(streams_of[5], (H, D), H ** -0.5, 0.09375, ((0, 8), (1, 16)))
    return {"tokens": tokens, "in_weight": in_weight, "short_filter": short_filter, "mr_filter": mr_filter, "mr_bias": mr_bias, "out_weight": out_weight}


def reference(tokens, in_weight, short_filter, mr_filter, mr_bias, out_weight):
    projected = jnp.dot(tokens, in_weight.reshape(D, 3 * H), preferred_element_type=jnp.float32)
    projected = projected.astype(jnp.bfloat16).reshape(TOKENS, 3, H).astype(jnp.float32)
    padded = jnp.pad(projected, ((2, 0), (0, 0), (0, 0)))
    featured = short_filter[0] * padded[2:] + short_filter[1] * padded[1:-1] + short_filter[2] * padded[:-2]
    product = (featured[:, 1, :] * featured[:, 2, :]).astype(jnp.bfloat16).astype(jnp.float32)
    channel_taps = jnp.repeat(mr_filter, GS, axis=1)
    product_padded = jnp.pad(product, ((KM - 1, 0), (0, 0)))

    def add_tap(lag_index, accumulated):
        window = lax.dynamic_slice_in_dim(product_padded, KM - 1 - lag_index, TOKENS, 0)
        return accumulated + channel_taps[lag_index] * window

    filtered = lax.fori_loop(0, KM, add_tap, jnp.zeros((TOKENS, H), jnp.float32))
    gated = (featured[:, 0, :] * (filtered + mr_bias * product)).astype(jnp.bfloat16)
    channel_block = H // N_TP

    def add_block(group_index, accumulated):
        gated_block = lax.dynamic_slice_in_dim(gated, group_index * channel_block, channel_block, 1)
        weight_block = lax.dynamic_slice_in_dim(out_weight, group_index * channel_block, channel_block, 0)
        block_sum = jnp.dot(gated_block, weight_block, preferred_element_type=jnp.float32).astype(jnp.bfloat16)
        return accumulated + lax.optimization_barrier(block_sum).astype(jnp.float32)

    mixed = lax.fori_loop(0, N_TP, add_block, jnp.zeros((TOKENS, D), jnp.float32))
    return mixed.astype(jnp.bfloat16)
```

```python
import functools

import jax
import jax.numpy as jnp
from jax import lax
from jax.experimental import pallas as pl
from jax.experimental.pallas import tpu as pltpu
from jax.sharding import Mesh, PartitionSpec as P

F32 = jnp.float32
BF16 = jnp.bfloat16
SHIFTS = (0, 1, -1, 2)
VM = pl.BlockSpec(memory_space=pltpu.VMEM)
SM = pl.BlockSpec(memory_space=pltpu.SMEM)
HB = pl.BlockSpec(memory_space=pl.ANY)
MIB = 1024 * 1024


def take(shard, axis, by):
    count = lax.axis_size(axis)
    return lax.ppermute(shard, axis, [((i + by) % count, i) for i in range(count)])


def give(shard, axis, by):
    count = lax.axis_size(axis)
    return lax.ppermute(shard, axis, [(i, (i + by) % count) for i in range(count)])


def call(body, out, name, ins, scratch=(), cost=(0, 0), **extra):
    return pl.pallas_call(
        body,
        out_shape=out,
        scratch_shapes=list(scratch),
        name=name,
        cost_estimate=pl.CostEstimate(flops=cost[0], bytes_accessed=cost[1], transcendentals=0),
        compiler_params=pltpu.CompilerParams(vmem_limit_bytes=48 * MIB),
        **extra,
    )(*ins)


def shape(*sizes, dtype=BF16):
    return jax.ShapeDtypeStruct(sizes, dtype)


def bands_kernel(base, out):
    groups, width = base.shape
    taps = width // 2
    for g in range(groups):
        row = jnp.broadcast_to(base[g : g + 1, :], (taps, width))
        out[g * taps : (g + 1) * taps, :] = pltpu.roll(
            row, 0, 1, stride=1, stride_axis=0
        ).astype(BF16)


def three_taps(work, taps, stream, rows):
    return (
        taps[stream : stream + 1, :] * work[8 : 8 + rows, :]
        + taps[3 + stream : 4 + stream, :] * work[7 : 7 + rows, :]
        + taps[6 + stream : 7 + stream, :] * work[6 : 6 + rows, :]
    )


def project_kernel(first, last, steps, tile, place, *refs):
    pieces = refs[:8]
    weight = refs[8]
    at = 9
    if not first:
        before = refs[at]
        at += 1
    if last:
        taps = refs[at]
        out, edge, rows, total, work = refs[at + 1 :]
    else:
        out, rows, total = refs[at:]
    step = pl.program_id(0)

    @pl.when(step == 0)
    def _():
        for n, shift in enumerate(SHIFTS):
            for c in range(2):
                z = lax.rem(place[0] + shift + 4, 4)
                core = place[1] if c == 0 else 1 - place[1]
                row = pl.multiple_of(z * 64 + core * 32, 32)
                for k in range(steps):
                    rows[k, pl.ds(row, 32), :] = pieces[2 * n + c][:, k * tile : (k + 1) * tile]
        if first:
            total[...] = jnp.zeros_like(total)
        else:
            total[...] = before[...]

    left = rows[step]
    for s in range(3):
        total[:, s * 512 : (s + 1) * 512] += jnp.dot(
            left, weight[s], preferred_element_type=F32
        )

    @pl.when(step == steps - 1)
    def _():
        if not last:
            out[...] = total[...]
        else:
            projected = total[...].astype(BF16)
            out[...] = projected
            streams = []
            for s in (1, 2):
                work[...] = projected[112:256, s * 512 : (s + 1) * 512].astype(F32)[8:, :]
                streams.append(three_taps(work, taps, s, 128))
            edge[0:128, :] = (streams[0] * streams[1]).astype(BF16)
            for s in range(3):
                edge[128 + 16 * s : 144 + 16 * s, :] = projected[
                    240:256, s * 512 : (s + 1) * 512
                ]


def project(place, pieces, weight, chunk, chunks, before, taps):
    depth = weight.shape[1] // chunks
    tile = 512
    steps = depth // tile
    first, last = chunk == 0, chunk == chunks - 1
    ins = [place, *pieces, weight]
    specs = [SM] + [pl.BlockSpec((32, depth), lambda k: (0, 0))] * 8
    specs.append(pl.BlockSpec((3, tile, 512), lambda k: (0, k + chunk * steps, 0)))
    if not first:
        ins.append(before)
        specs.append(pl.BlockSpec((256, 1536), lambda k: (0, 0)))
    scratch = [pltpu.VMEM((steps, 256, tile), BF16), pltpu.VMEM((256, 1536), F32)]
    if last:
        ins.append(taps)
        specs.append(pl.BlockSpec((9, 512), lambda k: (0, 0)))
        out = (shape(256, 1536), shape(176, 512))
        out_specs = (
            pl.BlockSpec((256, 1536), lambda k: (0, 0)),
            pl.BlockSpec((176, 512), lambda k: (0, 0)),
        )
        scratch.append(pltpu.VMEM((136, 512), F32))
    else:
        out = shape(256, 1536, dtype=F32)
        out_specs = pl.BlockSpec((256, 1536), lambda k: (0, 0))
    return call(
        functools.partial(project_kernel, first, last, steps, tile),
        out,
        "project",
        ins,
        scratch,
        (2 * 256 * depth * 1536, depth * 3072 + 4 * MIB),
        grid=(steps,),
        in_specs=specs,
        out_specs=out_specs,
    )


def mix_kernel(projected, edge, taps, bias, bands, out, work, window, query):
    streams = []
    for s in range(3):
        work[0:8, :] = edge[128 + 16 * s : 144 + 16 * s, :].astype(F32)[8:16, :]
        work[8:264, :] = projected[:, s * 512 : (s + 1) * 512].astype(F32)
        featured = three_taps(work, taps, s, 256)
        if s == 0:
            query[...] = featured
        else:
            streams.append(featured)
    product = (streams[0] * streams[1]).astype(BF16)
    window[0:128, :] = edge[0:128, :]
    window[128:384, :] = product
    lane = lax.broadcasted_iota(jnp.int32, (128, 128), 1) // 16
    for j in range(4):
        columns = slice(j * 128, (j + 1) * 128)
        right = jnp.concatenate([window[0:256, columns], window[128:384, columns]], axis=1)
        result = jnp.dot(
            bands[j * 1024 : (j + 1) * 1024, :], right, preferred_element_type=F32
        )
        for block in range(2):
            filtered = jnp.zeros((128, 128), F32)
            for g in range(8):
                filtered = jnp.where(
                    lane == g,
                    result[g * 128 : (g + 1) * 128, block * 128 : (block + 1) * 128],
                    filtered,
                )
            rows = slice(block * 128, (block + 1) * 128)
            direct = window[128 + block * 128 : 256 + block * 128, columns].astype(F32)
            out[rows, columns] = (
                query[rows, columns] * (filtered + bias[:, columns] * direct)
            ).astype(BF16)


def out_kernel(place, own, partner, weight, o0, o1, o2, o3, left, held, sems):
    copies = []
    for n in range(16):
        copy = pltpu.make_async_copy(
            weight.at[n], held.at[n // 2, :, pl.ds((n % 2) * 128, 128)], sems.at[n]
        )
        copy.start()
        copies.append(copy)
    outs = (o0, o1, o2, o3)
    for n, shift in enumerate(SHIFTS):
        z = lax.rem(place[0] + shift + 4, 4)
        row = pl.multiple_of(z * 64, 64)
        left[n * 64 : (n + 1) * 64, 0:512] = own[pl.ds(row, 64), :]
        left[n * 64 : (n + 1) * 64, 512:1024] = partner[pl.ds(row, 64), :]
    for j in range(8):
        copies[2 * j].wait()
        copies[2 * j + 1].wait()
        result = jnp.dot(left[...], held[j], preferred_element_type=F32)
        for n in range(4):
            outs[n][:, j * 256 : (j + 1) * 256] = result[n * 64 : (n + 1) * 64].astype(BF16)


def sum_kernel(place, a, b, c, d, keep, send):
    mine = pl.multiple_of(place[1] * 32, 32)
    theirs = pl.multiple_of((1 - place[1]) * 32, 32)
    for out, row in ((keep, mine), (send, theirs)):
        rows = pl.ds(row, 32)
        out[...] = (
            a[rows, :].astype(F32)
            + b[rows, :].astype(F32)
            + c[rows, :].astype(F32)
            + d[rows, :].astype(F32)
        ).astype(BF16)


def place_kernel(place, k0, k1, y0, y1, out):
    for h, (kept, got) in enumerate(((k0, y0), (k1, y1))):
        for c in range(16):
            for source, core in ((kept, place[1]), (got, 1 - place[1])):
                column = pl.multiple_of(c * 512 + h * 128 + core * 256, 128)
                out[:, pl.ds(column, 128)] = source[:, c * 128 : (c + 1) * 128]


def shards(tokens, in_weight, short_filter, mr_filter, mr_bias, out_weight):
    core = lax.axis_index("core")
    place = jnp.stack([lax.axis_index("z"), core]).astype(jnp.int32)

    mine = lax.dynamic_slice(out_weight, (0, core * 256), (512, 256))
    other = lax.dynamic_slice(out_weight, (0, (1 - core) * 256), (512, 256))
    pair = jnp.concatenate([mine, take(other, "core", 1)], axis=0)
    gathered = [
        lax.all_gather(pair[:, h * 128 : (h + 1) * 128], ("x", "y"), axis=0, tiled=False)
        for h in range(2)
    ]

    reversed_taps = jnp.flip(mr_filter, 0).T
    base = jnp.pad(reversed_taps, ((0, 0), (1, 127)))
    bands = call(
        bands_kernel, shape(4096, 256), "bands", [base], cost=(0, 4 * MIB), in_specs=[VM], out_specs=VM
    )
    taps = short_filter.reshape(9, 512)

    weight = jnp.transpose(in_weight, (1, 0, 2))
    chunks = 2
    depth = tokens.shape[1] // chunks
    pieces = []
    for c in range(chunks):
        part = tokens[:, c * depth : (c + 1) * depth]
        got = [part] + [take(part, "z", by) for by in SHIFTS[1:]]
        pieces.append([q for block in got for q in (block, take(block, "core", 1))])
    total = None
    for c in range(chunks):
        total = project(place, pieces[c], weight, c, chunks, total, taps)
    projected, edge = total

    count = lax.axis_size(("x", "y"))
    earlier = lax.ppermute(edge, ("x", "y"), [(i, i + 1) for i in range(count - 1)])
    gated = call(
        mix_kernel,
        shape(256, 512),
        "mix",
        [projected, earlier, taps, mr_bias.reshape(1, 512), bands],
        [pltpu.VMEM((264, 512), F32), pltpu.VMEM((384, 512), BF16), pltpu.VMEM((256, 512), F32)],
        (2 * 4096 * 256 * 256, 4 * MIB),
        in_specs=[VM] * 5,
        out_specs=VM,
    )
    partner = take(gated, "core", 1)

    kept, got = [], []
    for h in range(2):
        partials = call(
            out_kernel,
            (shape(64, 2048),) * 4,
            "out",
            [place, gated, partner, gathered[h]],
            [
                pltpu.VMEM((256, 1024), BF16),
                pltpu.VMEM((8, 1024, 256), BF16),
                pltpu.SemaphoreType.DMA((16,)),
            ],
            (2 * 256 * 1024 * 2048, 6 * MIB),
            in_specs=[SM, VM, VM, HB],
            out_specs=(VM,) * 4,
        )
        arrived = [give(partials[n], "z", SHIFTS[n]) for n in range(1, 4)]
        keep, send = call(
            sum_kernel,
            (shape(32, 2048),) * 2,
            "sum",
            [place, partials[0], *arrived],
            cost=(0, 2 * MIB),
            in_specs=[SM] + [VM] * 4,
            out_specs=(VM, VM),
        )
        kept.append(keep)
        got.append(take(send, "core", 1))
    return call(
        place_kernel,
        shape(32, 8192),
        "place",
        [place, *kept, *got],
        cost=(0, MIB),
        in_specs=[SM] + [VM] * 4,
        out_specs=VM,
    )


def solution(mesh):
    grid = Mesh(mesh.devices.reshape(4, 4, 4, 2), ("x", "y", "z", "core"))
    channels = ("z", "core")
    context = ("x", "y")
    return jax.shard_map(
        shards,
        mesh=grid,
        in_specs=(
            P(context + channels, None),
            P(None, None, channels),
            P(None, None, channels),
            P(None, channels),
            P(channels),
            P(channels, context),
        ),
        out_specs=P(context + channels, None),
        check_vma=False,
    )
```

```python
import functools

import jax
import jax.numpy as jnp
from jax import lax
from jax.experimental import pallas as pl
from jax.experimental.pallas import tpu as pltpu
from jax.sharding import Mesh, PartitionSpec as P

F32 = jnp.float32
BF16 = jnp.bfloat16
SHIFTS = (0, 1, -1, 2)
VM = pl.BlockSpec(memory_space=pltpu.VMEM)
SM = pl.BlockSpec(memory_space=pltpu.SMEM)
HB = pl.BlockSpec(memory_space=pltpu.MemorySpace.HBM)
MIB = 1024 * 1024


def take(shard, axis, by):
    count = lax.axis_size(axis)
    return lax.ppermute(shard, axis, [((i + by) % count, i) for i in range(count)])


def give(shard, axis, by):
    count = lax.axis_size(axis)
    return lax.ppermute(shard, axis, [(i, (i + by) % count) for i in range(count)])


def step(shard, axis, by=1):
    count = lax.axis_size(axis)
    pairs = []
    for i in range(count):
        for core in range(2):
            source = (i + (by if core == 0 else -by)) % count
            pairs.append((source * 2 + core, i * 2 + core))
    return lax.ppermute(shard, (axis, "core"), pairs)


def call(body, out, name, ins, scratch=(), cost=(0, 0), room=8, **extra):
    return pl.pallas_call(
        body,
        out_shape=out,
        scratch_shapes=list(scratch),
        name=name,
        cost_estimate=pl.CostEstimate(flops=cost[0], bytes_accessed=cost[1], transcendentals=0),
        compiler_params=pltpu.CompilerParams(vmem_limit_bytes=room * MIB),
        **extra,
    )(*ins)


def shape(*sizes, dtype=BF16):
    return jax.ShapeDtypeStruct(sizes, dtype)


def bands_kernel(filters, short, bias, out, taps, direct):
    groups, count = filters.shape
    lag = lax.broadcasted_iota(jnp.int32, (count, 2 * count), 0)
    column = lax.broadcasted_iota(jnp.int32, (count, 2 * count), 1)
    turned = (lag + column == count).astype(BF16)
    base = jnp.dot(filters[...].astype(BF16), turned, preferred_element_type=F32)
    for g in range(groups):
        row = jnp.broadcast_to(base[g : g + 1, :], (count, 2 * count))
        out[g * count : (g + 1) * count, :] = pltpu.roll(
            row, 0, 1, stride=1, stride_axis=0
        ).astype(BF16)
    for j in range(3):
        taps[3 * j : 3 * j + 3, :] = short[j]
    direct[...] = bias[...]


def three_taps(work, taps, stream, rows):
    return (
        taps[stream : stream + 1, :] * work[8 : 8 + rows, :]
        + taps[3 + stream : 4 + stream, :] * work[7 : 7 + rows, :]
        + taps[6 + stream : 7 + stream, :] * work[6 : 6 + rows, :]
    )


def project_kernel(place, *refs):
    pieces = refs[:8]
    weight, taps, out, edge, total, held, work, sems = refs[8:]
    slots, _, tile, _ = held.shape
    steps = weight.shape[1] // tile

    def fetch(k):
        slot = lax.rem(k, slots)
        rows = pl.ds(pl.multiple_of(k * tile, tile), tile)
        return pltpu.make_async_copy(weight.at[:, rows, :], held.at[slot], sems.at[slot])

    for k in range(slots):
        fetch(k).start()
    total[...] = jnp.zeros_like(total)

    @pl.loop(0, steps)
    def _(k):
        depth = pl.ds(pl.multiple_of(k * tile, tile), tile)
        left = jnp.concatenate([piece[:, depth] for piece in pieces], axis=0)
        fetch(k).wait()
        slot = lax.rem(k, slots)
        for s in range(3):
            total[:, s * 512 : (s + 1) * 512] += jnp.dot(
                left, held[slot, s], preferred_element_type=F32
            )

        @pl.when(k + slots < steps)
        def _():
            fetch(k + slots).start()

    sign = 1 - 2 * place[1]
    for n in range(4):
        for c in range(2):
            z = lax.rem(place[0] + (sign * n if c == 0 else -sign * n) + 4, 4)
            core = place[1] if c == 0 else 1 - place[1]
            row = pl.multiple_of(z * 64 + core * 32, 32)
            at = (2 * n + c) * 32
            out[pl.ds(row, 32), :] = total[at : at + 32, :].astype(BF16)
    streams = []
    for s in (1, 2):
        work[...] = out[112:256, s * 512 : (s + 1) * 512].astype(F32)[8:, :]
        streams.append(three_taps(work, taps, s, 128))
    edge[0:128, :] = (streams[0] * streams[1]).astype(BF16)
    for s in range(3):
        edge[128 + 16 * s : 144 + 16 * s, :] = out[240:256, s * 512 : (s + 1) * 512]


def mix_kernel(projected, edge, taps, bias, bands, out, work, window, query):
    streams = []
    for s in range(3):
        work[0:8, :] = edge[128 + 16 * s : 144 + 16 * s, :].astype(F32)[8:16, :]
        work[8:264, :] = projected[:, s * 512 : (s + 1) * 512].astype(F32)
        featured = three_taps(work, taps, s, 256)
        if s == 0:
            query[...] = featured
        else:
            streams.append(featured)
    product = (streams[0] * streams[1]).astype(BF16)
    window[0:128, :] = edge[0:128, :]
    window[128:384, :] = product
    lane = lax.broadcasted_iota(jnp.int32, (128, 128), 1) // 16
    for j in range(4):
        columns = slice(j * 128, (j + 1) * 128)
        right = jnp.concatenate([window[0:256, columns], window[128:384, columns]], axis=1)
        result = jnp.dot(
            bands[j * 1024 : (j + 1) * 1024, :], right, preferred_element_type=F32
        )
        for block in range(2):
            filtered = jnp.zeros((128, 128), F32)
            for g in range(8):
                filtered = jnp.where(
                    lane == g,
                    result[g * 128 : (g + 1) * 128, block * 128 : (block + 1) * 128],
                    filtered,
                )
            rows = slice(block * 128, (block + 1) * 128)
            direct = window[128 + block * 128 : 256 + block * 128, columns].astype(F32)
            out[rows, columns] = (
                query[rows, columns] * (filtered + bias[:, columns] * direct)
            ).astype(BF16)


def out_kernel(count, place, own, partner, *refs):
    groups = refs[:count]
    outs = refs[count : count + 4]
    left = refs[-1]
    for n, shift in enumerate(SHIFTS):
        z = lax.rem(place[0] + shift + 4, 4)
        row = pl.multiple_of(z * 64, 64)
        left[n * 64 : (n + 1) * 64, 0:512] = own[pl.ds(row, 64), :]
        left[n * 64 : (n + 1) * 64, 512:1024] = partner[pl.ds(row, 64), :]
    for j in range(2 * count):
        group, m = groups[j // 2], 2 * (j % 2)
        right = jnp.concatenate([group[m], group[m + 1]], axis=1)
        result = jnp.dot(left[...], right, preferred_element_type=F32)
        for n in range(4):
            outs[n][:, j * 256 : (j + 1) * 256] = result[n * 64 : (n + 1) * 64].astype(BF16)


def sum_kernel(place, a, b, c, d, keep, send):
    mine = pl.multiple_of(place[1] * 32, 32)
    theirs = pl.multiple_of((1 - place[1]) * 32, 32)
    for out, row in ((keep, mine), (send, theirs)):
        rows = pl.ds(row, 32)
        out[...] = (
            a[rows, :].astype(F32)
            + b[rows, :].astype(F32)
            + c[rows, :].astype(F32)
            + d[rows, :].astype(F32)
        ).astype(BF16)


def place_kernel(plan, place, *refs):
    out = refs[-1]
    for h, groups in enumerate(plan):
        for m in range(2):
            source = refs[2 * h + m]
            core = place[1] if m == 0 else 1 - place[1]
            sign = 1 - 2 * core
            for g, (half, far) in enumerate(groups):
                for near in range(4):
                    x_by, y_by = (near, far) if half == 0 else (far, near)
                    x = lax.rem(place[2] + sign * x_by + 4, 4)
                    y = lax.rem(place[3] + sign * y_by + 4, 4)
                    column = (x * 4 + y) * 512 + core * 256 + half * 128
                    at = (4 * g + near) * 128
                    out[:, pl.ds(pl.multiple_of(column, 128), 128)] = source[:, at : at + 128]


def ring(block, axis, steps):
    blocks = [block]
    for _ in range(steps):
        blocks.append(step(blocks[-1], axis))
    return blocks


def spread(block, half, near, far):
    own = jnp.stack(ring(block, near, 3))
    ahead = step(own, far)
    behind = step(own, far, -1)
    return [(half, 0, own), (half, 1, ahead), (half, -1, behind), (half, 2, step(ahead, far))]


def shards(tokens, in_weight, short_filter, mr_filter, mr_bias, out_weight):
    core = lax.axis_index("core")
    place = jnp.stack(
        [lax.axis_index("z"), core, lax.axis_index("x"), lax.axis_index("y")]
    ).astype(jnp.int32)

    pieces = []
    for block in ring(tokens, "z", 3):
        pieces += [block, take(block, "core", 1)]

    mine = lax.dynamic_slice(out_weight, (0, core * 256), (512, 256))
    other = lax.dynamic_slice(out_weight, (0, (1 - core) * 256), (512, 256))
    pair = jnp.concatenate([mine, take(other, "core", 1)], axis=0)
    one = spread(pair[:, :128], 0, "x", "y")
    two = spread(pair[:, 128:], 1, "y", "x")

    bands, taps, direct = call(
        bands_kernel,
        (shape(4096, 256), shape(9, 512, dtype=F32), shape(1, 512, dtype=F32)),
        "bands",
        [mr_filter.T, short_filter, mr_bias.reshape(1, 512)],
        cost=(0, 4 * MIB),
        in_specs=[VM] * 3,
        out_specs=(VM,) * 3,
    )

    weight = pltpu.with_memory_space_constraint(
        jnp.transpose(in_weight, (1, 0, 2)), pltpu.MemorySpace.HBM
    )
    projected, edge = call(
        project_kernel,
        (shape(256, 1536), shape(176, 512)),
        "project",
        [place, *pieces, weight, taps],
        [
            pltpu.VMEM((256, 1536), F32),
            pltpu.VMEM((6, 3, 512, 512), BF16),
            pltpu.VMEM((136, 512), F32),
            pltpu.SemaphoreType.DMA((6,)),
        ],
        (2 * 256 * 8192 * 1536, 28 * MIB),
        24,
        in_specs=[SM] + [VM] * 8 + [HB, VM],
        out_specs=(VM, VM),
    )

    context = ("x", "y")
    count = lax.axis_size(context)
    earlier = lax.ppermute(edge, context, [(i, i + 1) for i in range(count - 1)])
    gated = call(
        mix_kernel,
        shape(256, 512),
        "mix",
        [projected, earlier, taps, direct, bands],
        [pltpu.VMEM((264, 512), F32), pltpu.VMEM((384, 512), BF16), pltpu.VMEM((256, 512), F32)],
        (2 * 4096 * 256 * 256, 4 * MIB),
        in_specs=[VM] * 5,
        out_specs=VM,
    )
    partner = take(gated, "core", 1)

    parts = []
    plan = []
    for groups in (one[:3] + two[:3], one[3:] + two[3:]):
        width = 512 * len(groups)
        partials = call(
            functools.partial(out_kernel, len(groups)),
            (shape(64, width),) * 4,
            "out",
            [place, gated, partner] + [group[2] for group in groups],
            [pltpu.VMEM((256, 1024), BF16)],
            (2 * 256 * 1024 * width, 1024 * width * 2),
            in_specs=[SM] + [VM] * (2 + len(groups)),
            out_specs=(VM,) * 4,
        )
        arrived = [give(partials[m], "z", SHIFTS[m]) for m in range(1, 4)]
        keep, send = call(
            sum_kernel,
            (shape(32, width),) * 2,
            "sum",
            [place, partials[0], *arrived],
            cost=(0, 600 * width),
            in_specs=[SM] + [VM] * 4,
            out_specs=(VM, VM),
        )
        parts += [keep, take(send, "core", 1)]
        plan.append(tuple(group[:2] for group in groups))
    return call(
        functools.partial(place_kernel, tuple(plan)),
        shape(32, 8192),
        "place",
        [place, *parts],
        cost=(0, MIB),
        in_specs=[SM] + [VM] * len(parts),
        out_specs=VM,
    )


def solution(mesh):
    grid = Mesh(mesh.devices.reshape(4, 4, 4, 2), ("x", "y", "z", "core"))
    channels = ("z", "core")
    context = ("x", "y")
    return jax.shard_map(
        shards,
        mesh=grid,
        in_specs=(
            P(context + channels, None),
            P(None, None, channels),
            P(None, None, channels),
            P(None, channels),
            P(channels),
            P(channels, context),
        ),
        out_specs=P(context + channels, None),
        check_vma=False,
    )
```

```python
import functools

import jax
import jax.numpy as jnp
from jax import lax
from jax.experimental import pallas as pl
from jax.experimental.pallas import tpu as pltpu
from jax.sharding import Mesh, PartitionSpec as P

F32 = jnp.float32
BF16 = jnp.bfloat16
VM = pl.BlockSpec(memory_space=pltpu.VMEM)
SM = pl.BlockSpec(memory_space=pltpu.SMEM)
ANY = pl.BlockSpec(memory_space=pl.ANY)
MIB = 1024 * 1024


def turn(shard, axis, by):
    count = lax.axis_size(axis)
    pairs = []
    for i in range(count):
        for core in range(2):
            source = (i + (by if core == 0 else -by)) % count
            pairs.append((source * 2 + core, i * 2 + core))
    return lax.ppermute(shard, (axis, "core"), pairs)


def from_ahead(shard, axis):
    return turn(shard, axis, 1)


def from_behind(shard, axis):
    return turn(shard, axis, -1)


def cross(shard, axes, by):
    sizes = [lax.axis_size(axis) for axis in ("x", "y")]
    pairs = []
    for i in range(sizes[0]):
        for j in range(sizes[1]):
            for core in range(2):
                source = {"x": i, "y": j}
                source[axes[core]] = (source[axes[core]] + by) % sizes[0]
                pairs.append((((source["x"] * sizes[1]) + source["y"]) * 2 + core, (i * sizes[1] + j) * 2 + core))
    return lax.ppermute(shard, ("x", "y", "core"), pairs)


def swap(shard):
    return lax.ppermute(shard, "core", [(0, 1), (1, 0)])


def call(body, out, name, ins, scratch=(), cost=(0, 0), room=8, **extra):
    return pl.pallas_call(
        body,
        out_shape=out,
        scratch_shapes=list(scratch),
        name=name,
        cost_estimate=pl.CostEstimate(flops=cost[0], bytes_accessed=cost[1], transcendentals=0),
        compiler_params=pltpu.CompilerParams(vmem_limit_bytes=room * MIB),
        **extra,
    )(*ins)


def shape(*sizes, dtype=BF16):
    return jax.ShapeDtypeStruct(sizes, dtype)


def in_vmem(array):
    return pltpu.with_memory_space_constraint(array, pltpu.VMEM)


def in_hbm(array):
    return pltpu.with_memory_space_constraint(array, pltpu.MemorySpace.HBM)


def make_bands(filters, out):
    groups, count = filters.shape
    lag = lax.broadcasted_iota(jnp.int32, (count, 2 * count), 0)
    column = lax.broadcasted_iota(jnp.int32, (count, 2 * count), 1)
    turned = (lag + column == count).astype(BF16)
    base = jnp.dot(filters[...].astype(BF16), turned, preferred_element_type=F32)
    for g in range(groups):
        row = jnp.broadcast_to(base[g : g + 1, :], (count, 2 * count))
        out[g * count : (g + 1) * count, :] = pltpu.roll(
            row, 0, 1, stride=1, stride_axis=0
        ).astype(BF16)


def three_taps(work, taps, stream, rows):
    return (
        taps[0, stream : stream + 1, :] * work[8 : 8 + rows, :]
        + taps[1, stream : stream + 1, :] * work[7 : 7 + rows, :]
        + taps[2, stream : stream + 1, :] * work[6 : 6 + rows, :]
    )


def project_kernel(half, place, *refs):
    pieces, weight = refs[:8], refs[8]
    if half == 0:
        filters, short, bias = refs[9:12]
        total, bands, taps, direct = refs[12:16]
        rows, held, row_sems, weight_sems, small, small_sems = refs[16:]
    else:
        before, taps = refs[9:11]
        out, edge = refs[-8:-6]
        rows, held, row_sems, weight_sems, total, work = refs[-6:]
    slots, _, tile, _ = held.shape
    parts, _, span = rows.shape
    per_part = span // tile
    steps = parts * per_part
    sign = 1 - 2 * place[1]

    def bring(n, t):
        far = sign * (n // 2)
        z = lax.rem(place[0] + (far if n % 2 == 0 else -far) + 4, 4)
        core = place[1] if n % 2 == 0 else 1 - place[1]
        row = pl.ds(pl.multiple_of(z * 64 + core * 32, 32), 32)
        depth = pl.ds((half * parts + t) * span, span)
        return pltpu.make_async_copy(pieces[n].at[:, depth], rows.at[t, row, :], row_sems.at[n, t])

    def fetch(k):
        depth = pl.ds((half * steps + k) * tile, tile)
        return pltpu.make_async_copy(
            weight.at[:, depth, :], held.at[k % slots], weight_sems.at[k % slots]
        )

    for n in range(8):
        bring(n, 0).start()
    for k in range(slots):
        fetch(k).start()
    if half == 0:
        little = [
            pltpu.make_async_copy(source, target, small_sems.at[n])
            for n, (source, target) in enumerate(((filters, small), (short, taps), (bias, direct)))
        ]
        for copy in little:
            copy.start()
    for t in range(1, parts):
        for n in range(8):
            bring(n, t).start()
    if half == 0:
        for copy in little:
            copy.wait()
        make_bands(small, bands)
        total[...] = jnp.zeros_like(total)
    else:
        total[...] = before[...]

    for t in range(parts):
        for n in range(8):
            bring(n, t).wait()
        for u in range(per_part):
            k = t * per_part + u
            fetch(k).wait()
            left = rows[t, :, u * tile : (u + 1) * tile]
            for s in range(3):
                total[:, s * 512 : (s + 1) * 512] += jnp.dot(
                    left, held[k % slots, s], preferred_element_type=F32
                )
            if k + slots < steps:
                fetch(k + slots).start()

    if half == 1:
        out[...] = total[...].astype(BF16)
        streams = []
        for s in (1, 2):
            work[...] = out[112:256, s * 512 : (s + 1) * 512].astype(F32)[8:, :]
            streams.append(three_taps(work, taps, s, 128))
        edge[0:128, :] = (streams[0] * streams[1]).astype(BF16)
        for s in range(3):
            edge[128 + 16 * s : 144 + 16 * s, :] = out[240:256, s * 512 : (s + 1) * 512]


def mix_kernel(projected, edge, taps, bias, bands, one, two, out, work, window, query):
    streams = []
    for s in range(3):
        work[0:8, :] = edge[128 + 16 * s : 144 + 16 * s, :].astype(F32)[8:16, :]
        work[8:264, :] = projected[:, s * 512 : (s + 1) * 512].astype(F32)
        featured = three_taps(work, taps, s, 256)
        if s == 0:
            query[...] = featured
        else:
            streams.append(featured)
    product = (streams[0] * streams[1]).astype(BF16)
    window[0:128, :] = edge[0:128, :]
    window[128:384, :] = product
    lane = lax.broadcasted_iota(jnp.int32, (128, 128), 1) // 16
    for j in range(4):
        columns = slice(j * 128, (j + 1) * 128)
        right = jnp.concatenate([window[0:256, columns], window[128:384, columns]], axis=1)
        result = jnp.dot(
            bands[j * 1024 : (j + 1) * 1024, :], right, preferred_element_type=F32
        )
        for block in range(2):
            filtered = jnp.zeros((128, 128), F32)
            for g in range(8):
                filtered = jnp.where(
                    lane == g,
                    result[g * 128 : (g + 1) * 128, block * 128 : (block + 1) * 128],
                    filtered,
                )
            rows = slice(block * 128, (block + 1) * 128)
            direct = window[128 + block * 128 : 256 + block * 128, columns].astype(F32)
            out[rows, columns] = (
                query[rows, columns] * (filtered + bias[:, columns] * direct)
            ).astype(BF16)


def out_kernel(count, blocks, place, gated, *refs):
    groups = refs[:count]
    keep, send, left = refs[count:]
    for m in range(2):
        core = place[1] if m == 0 else 1 - place[1]
        sign = 1 - 2 * core
        for n, by in enumerate((0, 1, -1, 2)):
            z = lax.rem(place[0] + sign * by + 4, 4)
            row = pl.multiple_of(z * 64 + core * 32, 32)
            at = m * 128 + n * 32
            left[at : at + 32, :] = gated[pl.ds(row, 32), :]
    labels = [block[0] for block in blocks]
    for at, ((near, far), group, n) in enumerate(blocks):
        result = jnp.dot(left[...], groups[group][n], preferred_element_type=F32).astype(BF16)
        to = labels.index((far, near))
        keep[:, at * 512 : (at + 1) * 512] = result[0:128]
        send[:, to * 512 : (to + 1) * 512] = result[128:256]


def pair_kernel(kept, got, *outs):
    for n, out in enumerate(outs):
        rows = slice(32 * n, 32 * (n + 1))
        out[...] = (kept[rows, :].astype(F32) + got[rows, :].astype(F32)).astype(BF16)


def join_kernel(a, b, out):
    out[...] = (a[...].astype(F32) + b[...].astype(F32)).astype(BF16)


def finish_kernel(plan, place, *refs):
    out = refs[-1]
    for h, labels in enumerate(plan):
        parts = refs[3 * h : 3 * h + 3]
        for n, (near, far) in enumerate(labels):
            x = lax.rem(place[2] + jnp.where(place[1] == 0, near, far) + 4, 4)
            y = lax.rem(place[3] + jnp.where(place[1] == 0, far, near) + 4, 4)
            column = pl.multiple_of((x * 4 + y) * 512, 512)
            at = slice(n * 512, (n + 1) * 512)
            total = parts[0][:, at].astype(F32)
            for part in parts[1:]:
                total += part[:, at].astype(F32)
            out[:, pl.ds(column, 512)] = total.astype(BF16)


def stack_kernel(count, *refs):
    sources, out, sems = refs[:count], refs[-2], refs[-1]
    copies = [
        pltpu.make_async_copy(source, out.at[n], sems.at[n]) for n, source in enumerate(sources)
    ]
    for copy in copies:
        copy.start()
    for copy in copies:
        copy.wait()


def stacked(arrays, after):
    count = len(arrays)
    return call(
        functools.partial(stack_kernel, count),
        shape(count, *arrays[0].shape),
        "stack",
        [*arrays, *after],
        [pltpu.SemaphoreType.DMA((count,))],
        (0, count * MIB),
        in_specs=[ANY] * (count + len(after)),
        out_specs=VM,
    )


def halves_kernel(ahead, behind, after, one, two, sems):
    copies = [
        pltpu.make_async_copy(ahead.at[pl.ds(0, 2)], one, sems.at[0]),
        pltpu.make_async_copy(behind.at[pl.ds(2, 2)], two, sems.at[1]),
    ]
    for copy in copies:
        copy.start()
    for copy in copies:
        copy.wait()


NEAR, FAR = ("x", "y"), ("y", "x")


def spread(block, after):
    blocks = [block] + [cross(block, NEAR, by) for by in (1, -1, 2)]
    own = stacked([in_hbm(block)] + [in_vmem(block) for block in blocks[1:]], after)
    return [own] + [cross(own, FAR, by) for by in (1, -1)]


def shards(tokens, in_weight, short_filter, mr_filter, mr_bias, out_weight):
    place = jnp.stack([lax.axis_index(a) for a in ("z", "core", "x", "y")]).astype(jnp.int32)

    pieces = []
    ahead = from_ahead(tokens, "z")
    for block in (tokens, ahead, from_ahead(ahead, "z"), from_behind(tokens, "z")):
        pieces += [block, swap(block)]
    pieces = [in_hbm(tokens)] + [in_vmem(piece) for piece in pieces[1:]]

    weights = spread(out_weight, [pieces[2], pieces[6]])

    weight = in_hbm(jnp.transpose(in_weight, (1, 0, 2)))
    parts, span, slots = 2, 2048, 5
    scratch = [
        pltpu.VMEM((parts, 256, span), BF16),
        pltpu.VMEM((slots, 3, 512, 512), BF16),
        pltpu.SemaphoreType.DMA((8, parts)),
        pltpu.SemaphoreType.DMA((slots,)),
    ]
    cost = (256 * 8192 * 1536, 14 * MIB)
    total, bands, taps, direct = call(
        functools.partial(project_kernel, 0),
        (
            shape(256, 1536, dtype=F32),
            shape(4096, 256),
            shape(3, 3, 512, dtype=F32),
            shape(1, 512, dtype=F32),
        ),
        "project",
        [
            place,
            *pieces,
            weight,
            in_hbm(mr_filter.T),
            in_hbm(short_filter),
            in_hbm(mr_bias.reshape(1, 512)),
        ],
        scratch + [pltpu.VMEM((32, 128), F32), pltpu.SemaphoreType.DMA((3,))],
        cost,
        16,
        in_specs=[SM] + [ANY] * 12,
        out_specs=(VM,) * 4,
    )
    relays = call(
        halves_kernel,
        (shape(2, 512, 512),) * 2,
        "halves",
        [*weights[1:], direct],
        [pltpu.SemaphoreType.DMA((2,))],
        (0, 4 * MIB),
        in_specs=[VM, VM, ANY],
        out_specs=(VM, VM),
    )
    weights += [cross(relays[0], FAR, 1), cross(relays[1], FAR, -1)]
    projected, edge = call(
        functools.partial(project_kernel, 1),
        (shape(256, 1536), shape(176, 512)),
        "project",
        [place, *pieces, weight, total, taps, relays[0]],
        scratch + [pltpu.VMEM((256, 1536), F32), pltpu.VMEM((136, 512), F32)],
        cost,
        18,
        in_specs=[SM] + [ANY] * 9 + [VM, VM, ANY],
        out_specs=(VM, VM),
    )

    context = ("x", "y")
    count = lax.axis_size(context)
    earlier = lax.ppermute(edge, context, [(i, i + 1) for i in range(count - 1)])
    gated = call(
        mix_kernel,
        shape(256, 512),
        "mix",
        [projected, earlier, taps, direct, bands, *weights[3:]],
        [pltpu.VMEM((264, 512), F32), pltpu.VMEM((384, 512), BF16), pltpu.VMEM((256, 512), F32)],
        (2 * 4096 * 256 * 256, 4 * MIB),
        in_specs=[VM] * 5 + [ANY] * 2,
        out_specs=VM,
    )

    steps = (0, 1, -1, 2)
    chunks = (
        (weights[:3], [((n, f), g, m) for g, f in enumerate(steps[:3]) for m, n in enumerate(steps[:3])]),
        (
            weights,
            [((2, f), g, 3) for g, f in enumerate(steps[:3])]
            + [((n, 2), 3 + m // 2, m % 2) for m, n in enumerate(steps)],
        ),
    )
    sums = []
    plan = []
    for groups, blocks in chunks:
        width = 512 * len(blocks)
        keep, send = call(
            functools.partial(out_kernel, len(groups), blocks),
            (shape(128, width),) * 2,
            "out",
            [place, gated, *groups],
            [pltpu.VMEM((256, 512), BF16)],
            (2 * 256 * 512 * width, 512 * width * 2),
            in_specs=[SM] + [VM] * (1 + len(groups)),
            out_specs=(VM, VM),
        )
        here, front, back, across = call(
            pair_kernel,
            (shape(32, width),) * 4,
            "pair",
            [keep, swap(send)],
            cost=(0, 768 * width),
            in_specs=[VM, VM],
            out_specs=(VM,) * 4,
        )
        back = from_ahead(back, "z")
        joined = call(
            join_kernel,
            shape(32, width),
            "join",
            [front, from_behind(across, "z")],
            cost=(0, 192 * width),
            in_specs=[VM, VM],
            out_specs=VM,
        )
        parts = [here, back, from_behind(joined, "z")]
        sums += parts
        plan.append([block[0] for block in blocks])
    return call(
        functools.partial(finish_kernel, plan),
        shape(32, 8192),
        "finish",
        [place, *sums],
        cost=(0, 3 * MIB),
        in_specs=[SM] + [VM] * len(sums),
        out_specs=VM,
    )


def solution(mesh):
    grid = Mesh(mesh.devices.reshape(4, 4, 4, 2), ("x", "y", "z", "core"))
    channels = ("z", "core")
    context = ("x", "y")
    return jax.shard_map(
        shards,
        mesh=grid,
        in_specs=(
            P(context + channels, None),
            P(None, None, channels),
            P(None, None, channels),
            P(None, channels),
            P(channels),
            P(channels, context),
        ),
        out_specs=P(context + channels, None),
        check_vma=False,
    )
```

```python
import functools

import jax
import jax.numpy as jnp
from jax import lax
from jax.experimental import pallas as pl
from jax.experimental.pallas import tpu as pltpu
from jax.sharding import Mesh, PartitionSpec as P

F32 = jnp.float32
BF16 = jnp.bfloat16
VM = pl.BlockSpec(memory_space=pltpu.VMEM)
SM = pl.BlockSpec(memory_space=pltpu.SMEM)
ANY = pl.BlockSpec(memory_space=pl.ANY)
MIB = 1024 * 1024


def turn(shard, axis, by):
    count = lax.axis_size(axis)
    pairs = []
    for i in range(count):
        for core in range(2):
            source = (i + (by if core == 0 else -by)) % count
            pairs.append((source * 2 + core, i * 2 + core))
    return lax.ppermute(shard, (axis, "core"), pairs)


def from_ahead(shard, axis):
    return turn(shard, axis, 1)


def from_behind(shard, axis):
    return turn(shard, axis, -1)


def cross(shard, axes, by):
    sizes = [lax.axis_size(axis) for axis in ("x", "y")]
    pairs = []
    for i in range(sizes[0]):
        for j in range(sizes[1]):
            for core in range(2):
                source = {"x": i, "y": j}
                source[axes[core]] = (source[axes[core]] + by) % sizes[0]
                pairs.append((((source["x"] * sizes[1]) + source["y"]) * 2 + core, (i * sizes[1] + j) * 2 + core))
    return lax.ppermute(shard, ("x", "y", "core"), pairs)


def swap(shard):
    return lax.ppermute(shard, "core", [(0, 1), (1, 0)])


def call(body, out, name, ins, scratch=(), cost=(0, 0), room=8, **extra):
    return pl.pallas_call(
        body,
        out_shape=out,
        scratch_shapes=list(scratch),
        name=name,
        cost_estimate=pl.CostEstimate(flops=cost[0], bytes_accessed=cost[1], transcendentals=0),
        compiler_params=pltpu.CompilerParams(vmem_limit_bytes=room * MIB),
        **extra,
    )(*ins)


def shape(*sizes, dtype=BF16):
    return jax.ShapeDtypeStruct(sizes, dtype)


def in_vmem(array):
    return pltpu.with_memory_space_constraint(array, pltpu.VMEM)


def in_hbm(array):
    return pltpu.with_memory_space_constraint(array, pltpu.MemorySpace.HBM)


def make_bands(filters, out):
    groups, count = filters.shape
    lag = lax.broadcasted_iota(jnp.int32, (count, 2 * count), 0)
    column = lax.broadcasted_iota(jnp.int32, (count, 2 * count), 1)
    turned = (lag + column == count).astype(BF16)
    base = jnp.dot(filters[...].astype(BF16), turned, preferred_element_type=F32)
    for g in range(groups):
        row = jnp.broadcast_to(base[g : g + 1, :], (count, 2 * count))
        out[g * count : (g + 1) * count, :] = pltpu.roll(
            row, 0, 1, stride=1, stride_axis=0
        ).astype(BF16)


def three_taps(work, taps, stream, rows):
    return (
        taps[0, stream : stream + 1, :] * work[8 : 8 + rows, :]
        + taps[1, stream : stream + 1, :] * work[7 : 7 + rows, :]
        + taps[2, stream : stream + 1, :] * work[6 : 6 + rows, :]
    )


def project_kernel(half, done, place, *refs):
    pieces, weight = refs[:8], refs[8]
    if half == 0:
        filters, short, bias = refs[9:12]
        total, bands, taps, direct = refs[12:16]
        rows, held, row_sems, weight_sems, small, small_sems = refs[16:]
    else:
        before, taps = refs[9:11]
        out, edge = refs[-8:-6]
        rows, held, row_sems, weight_sems, total, work = refs[-6:]
    slots, _, tile, _ = held.shape
    parts, _, span = rows.shape
    per_part = span // tile
    steps = parts * per_part
    sign = 1 - 2 * place[1]

    def bring(n, t):
        far = sign * (n // 2)
        z = lax.rem(place[0] + (far if n % 2 == 0 else -far) + 4, 4)
        core = place[1] if n % 2 == 0 else 1 - place[1]
        row = pl.ds(pl.multiple_of(z * 64 + core * 32, 32), 32)
        depth = pl.ds((done + t) * span, span)
        return pltpu.make_async_copy(pieces[n].at[:, depth], rows.at[t, row, :], row_sems.at[n, t])

    def fetch(k):
        depth = pl.ds(done * span + k * tile, tile)
        return pltpu.make_async_copy(
            weight.at[:, depth, :], held.at[k % slots], weight_sems.at[k % slots]
        )

    for n in range(8):
        bring(n, 0).start()
    for k in range(slots):
        fetch(k).start()
    if half == 0:
        little = [
            pltpu.make_async_copy(source, target, small_sems.at[n])
            for n, (source, target) in enumerate(((filters, small), (short, taps), (bias, direct)))
        ]
        for copy in little:
            copy.start()
    for t in range(1, parts):
        for n in range(8):
            bring(n, t).start()
    if half == 0:
        for copy in little:
            copy.wait()
        make_bands(small, bands)
        total[...] = jnp.zeros_like(total)
    else:
        total[...] = before[...]

    for t in range(parts):
        for n in range(8):
            bring(n, t).wait()
        for u in range(per_part):
            k = t * per_part + u
            fetch(k).wait()
            left = rows[t, :, u * tile : (u + 1) * tile]
            for s in range(3):
                total[:, s * 512 : (s + 1) * 512] += jnp.dot(
                    left, held[k % slots, s], preferred_element_type=F32
                )
            if k + slots < steps:
                fetch(k + slots).start()

    if half == 1:
        out[...] = total[...].astype(BF16)
        streams = []
        for s in (1, 2):
            work[...] = out[112:256, s * 512 : (s + 1) * 512].astype(F32)[8:, :]
            streams.append(three_taps(work, taps, s, 128))
        edge[0:128, :] = (streams[0] * streams[1]).astype(BF16)
        for s in range(3):
            edge[128 + 16 * s : 144 + 16 * s, :] = out[240:256, s * 512 : (s + 1) * 512]


def mix_kernel(projected, edge, taps, bias, bands, one, two, out, work, window, query):
    streams = []
    for s in range(3):
        work[0:8, :] = edge[128 + 16 * s : 144 + 16 * s, :].astype(F32)[8:16, :]
        work[8:264, :] = projected[:, s * 512 : (s + 1) * 512].astype(F32)
        featured = three_taps(work, taps, s, 256)
        if s == 0:
            query[...] = featured
        else:
            streams.append(featured)
    product = (streams[0] * streams[1]).astype(BF16)
    window[0:128, :] = edge[0:128, :]
    window[128:384, :] = product
    lane = lax.broadcasted_iota(jnp.int32, (128, 128), 1) // 16
    for j in range(4):
        columns = slice(j * 128, (j + 1) * 128)
        right = jnp.concatenate([window[0:256, columns], window[128:384, columns]], axis=1)
        result = jnp.dot(
            bands[j * 1024 : (j + 1) * 1024, :], right, preferred_element_type=F32
        )
        for block in range(2):
            filtered = jnp.zeros((128, 128), F32)
            for g in range(8):
                filtered = jnp.where(
                    lane == g,
                    result[g * 128 : (g + 1) * 128, block * 128 : (block + 1) * 128],
                    filtered,
                )
            rows = slice(block * 128, (block + 1) * 128)
            direct = window[128 + block * 128 : 256 + block * 128, columns].astype(F32)
            out[rows, columns] = (
                query[rows, columns] * (filtered + bias[:, columns] * direct)
            ).astype(BF16)


def out_kernel(count, blocks, place, gated, *refs):
    groups = refs[:count]
    keep, send, left, held, sems = refs[count:]
    copies = [
        pltpu.make_async_copy(groups[group].at[n], held.at[at], sems.at[at])
        for at, (_, group, n) in enumerate(blocks)
    ]
    for copy in copies:
        copy.start()
    for m in range(2):
        core = place[1] if m == 0 else 1 - place[1]
        sign = 1 - 2 * core
        for n, by in enumerate((0, 1, -1, 2)):
            z = lax.rem(place[0] + sign * by + 4, 4)
            row = pl.multiple_of(z * 64 + core * 32, 32)
            at = m * 128 + n * 32
            left[at : at + 32, :] = gated[pl.ds(row, 32), :]
    labels = [block[0] for block in blocks]
    for at, (near, far) in enumerate(labels):
        copies[at].wait()
        result = jnp.dot(left[...], held[at], preferred_element_type=F32).astype(BF16)
        to = labels.index((far, near))
        keep[:, at * 512 : (at + 1) * 512] = result[0:128]
        send[:, to * 512 : (to + 1) * 512] = result[128:256]


def pair_kernel(kept, got, *outs):
    for n, out in enumerate(outs):
        rows = slice(32 * n, 32 * (n + 1))
        out[...] = (kept[rows, :].astype(F32) + got[rows, :].astype(F32)).astype(BF16)


def join_kernel(a, b, out):
    out[...] = (a[...].astype(F32) + b[...].astype(F32)).astype(BF16)


def finish_kernel(plan, place, *refs):
    out = refs[-1]
    for h, labels in enumerate(plan):
        parts = refs[3 * h : 3 * h + 3]
        for n, (near, far) in enumerate(labels):
            x = lax.rem(place[2] + jnp.where(place[1] == 0, near, far) + 4, 4)
            y = lax.rem(place[3] + jnp.where(place[1] == 0, far, near) + 4, 4)
            column = pl.multiple_of((x * 4 + y) * 512, 512)
            at = slice(n * 512, (n + 1) * 512)
            total = parts[0][:, at].astype(F32)
            for part in parts[1:]:
                total += part[:, at].astype(F32)
            out[:, pl.ds(column, 512)] = total.astype(BF16)


def stack_kernel(count, *refs):
    sources, out, sems = refs[:count], refs[-2], refs[-1]
    copies = [
        pltpu.make_async_copy(source, out.at[n], sems.at[n]) for n, source in enumerate(sources)
    ]
    for copy in copies:
        copy.start()
    for copy in copies:
        copy.wait()


def stacked(arrays, after):
    count = len(arrays)
    return call(
        functools.partial(stack_kernel, count),
        shape(count, *arrays[0].shape),
        "stack",
        [*arrays, *after],
        [pltpu.SemaphoreType.DMA((count,))],
        (0, count * MIB),
        in_specs=[ANY] * (count + len(after)),
        out_specs=VM,
    )


def halves_kernel(ahead, behind, after, one, two, sems):
    copies = []
    for n, (source, target) in enumerate(
        ((ahead.at[0], one.at[0]), (ahead.at[1], one.at[1]), (behind.at[2], two.at[0]), (behind.at[3], two.at[1]))
    ):
        copies.append(pltpu.make_async_copy(source, target, sems.at[n]))
        copies[-1].start()
    for copy in copies:
        copy.wait()


NEAR, FAR = ("x", "y"), ("y", "x")


def spread(block, after):
    blocks = [block] + [cross(block, NEAR, by) for by in (1, -1, 2)]
    own = stacked([in_hbm(block)] + [in_vmem(block) for block in blocks[1:]], after)
    return [own] + [in_hbm(cross(own, FAR, by)) for by in (1, -1)]


def shards(tokens, in_weight, short_filter, mr_filter, mr_bias, out_weight):
    place = jnp.stack([lax.axis_index(a) for a in ("z", "core", "x", "y")]).astype(jnp.int32)

    pieces = []
    ahead = from_ahead(tokens, "z")
    for block in (tokens, ahead, from_ahead(ahead, "z"), from_behind(tokens, "z")):
        pieces += [block, swap(block)]
    pieces = [in_hbm(tokens)] + [in_vmem(piece) for piece in pieces[1:]]

    weights = spread(out_weight, [pieces[2], pieces[6]])

    weight = in_hbm(jnp.transpose(in_weight, (1, 0, 2)))
    span, slots, first = 1024, 5, 5

    def room(parts):
        return [
            pltpu.VMEM((parts, 256, span), BF16),
            pltpu.VMEM((slots, 3, 512, 512), BF16),
            pltpu.SemaphoreType.DMA((8, parts)),
            pltpu.SemaphoreType.DMA((slots,)),
        ]

    cost = (256 * 8192 * 1536, 14 * MIB)
    total, bands, taps, direct = call(
        functools.partial(project_kernel, 0, 0),
        (
            shape(256, 1536, dtype=F32),
            shape(4096, 256),
            shape(3, 3, 512, dtype=F32),
            shape(1, 512, dtype=F32),
        ),
        "project",
        [
            place,
            *pieces,
            weight,
            in_hbm(mr_filter.T),
            in_hbm(short_filter),
            in_hbm(mr_bias.reshape(1, 512)),
        ],
        room(first) + [pltpu.VMEM((32, 128), F32), pltpu.SemaphoreType.DMA((3,))],
        cost,
        16,
        in_specs=[SM] + [ANY] * 12,
        out_specs=(VM,) * 4,
    )
    relays = call(
        halves_kernel,
        (shape(2, 512, 512),) * 2,
        "halves",
        [*weights[1:], direct],
        [pltpu.SemaphoreType.DMA((4,))],
        (0, 4 * MIB),
        in_specs=[ANY] * 3,
        out_specs=(VM, VM),
    )
    weights += [cross(relays[0], FAR, 1), cross(relays[1], FAR, -1)]
    projected, edge = call(
        functools.partial(project_kernel, 1, first),
        (shape(256, 1536), shape(176, 512)),
        "project",
        [place, *pieces, weight, total, taps, relays[0]],
        room(8 - first) + [pltpu.VMEM((256, 1536), F32), pltpu.VMEM((136, 512), F32)],
        cost,
        18,
        in_specs=[SM] + [ANY] * 9 + [VM, VM, ANY],
        out_specs=(VM, VM),
    )

    context = ("x", "y")
    count = lax.axis_size(context)
    earlier = lax.ppermute(edge, context, [(i, i + 1) for i in range(count - 1)])
    gated = call(
        mix_kernel,
        shape(256, 512),
        "mix",
        [projected, earlier, taps, direct, bands, *weights[3:]],
        [pltpu.VMEM((264, 512), F32), pltpu.VMEM((384, 512), BF16), pltpu.VMEM((256, 512), F32)],
        (2 * 4096 * 256 * 256, 4 * MIB),
        in_specs=[VM] * 5 + [ANY] * 2,
        out_specs=VM,
    )

    steps = (0, 1, -1, 2)
    chunks = (
        (weights[:3], [((n, f), g, m) for g, f in enumerate(steps[:3]) for m, n in enumerate(steps[:3])]),
        (
            weights,
            [((2, f), g, 3) for g, f in enumerate(steps[:3])]
            + [((n, 2), 3 + m // 2, m % 2) for m, n in enumerate(steps)],
        ),
    )
    sums = []
    plan = []
    for groups, blocks in chunks:
        width = 512 * len(blocks)
        keep, send = call(
            functools.partial(out_kernel, len(groups), blocks),
            (shape(128, width),) * 2,
            "out",
            [place, gated, *groups],
            [
                pltpu.VMEM((256, 512), BF16),
                pltpu.VMEM((len(blocks), 512, 512), BF16),
                pltpu.SemaphoreType.DMA((len(blocks),)),
            ],
            (2 * 256 * 512 * width, 512 * width * 2),
            10,
            in_specs=[SM, VM] + [ANY] * len(groups),
            out_specs=(VM, VM),
        )
        here, front, back, across = call(
            pair_kernel,
            (shape(32, width),) * 4,
            "pair",
            [keep, swap(send)],
            cost=(0, 768 * width),
            in_specs=[VM, VM],
            out_specs=(VM,) * 4,
        )
        back = from_ahead(back, "z")
        joined = call(
            join_kernel,
            shape(32, width),
            "join",
            [front, from_behind(across, "z")],
            cost=(0, 192 * width),
            in_specs=[VM, VM],
            out_specs=VM,
        )
        parts = [here, back, from_behind(joined, "z")]
        sums += parts
        plan.append([block[0] for block in blocks])
    return call(
        functools.partial(finish_kernel, plan),
        shape(32, 8192),
        "finish",
        [place, *sums],
        cost=(0, 3 * MIB),
        in_specs=[SM] + [VM] * len(sums),
        out_specs=VM,
    )


def solution(mesh):
    grid = Mesh(mesh.devices.reshape(4, 4, 4, 2), ("x", "y", "z", "core"))
    channels = ("z", "core")
    context = ("x", "y")
    return jax.shard_map(
        shards,
        mesh=grid,
        in_specs=(
            P(context + channels, None),
            P(None, None, channels),
            P(None, None, channels),
            P(None, channels),
            P(channels),
            P(channels, context),
        ),
        out_specs=P(context + channels, None),
        check_vma=False,
    )
```

```python
import functools

import jax
import jax.numpy as jnp
from jax import lax
from jax.experimental import pallas as pl
from jax.experimental.pallas import tpu as pltpu
from jax.sharding import Mesh, PartitionSpec as P

F32 = jnp.float32
BF16 = jnp.bfloat16
VM = pl.BlockSpec(memory_space=pltpu.VMEM)
SM = pl.BlockSpec(memory_space=pltpu.SMEM)
ANY = pl.BlockSpec(memory_space=pl.ANY)
MIB = 1024 * 1024


def turn(shard, axis, by):
    count = lax.axis_size(axis)
    pairs = []
    for i in range(count):
        for core in range(2):
            source = (i + (by if core == 0 else -by)) % count
            pairs.append((source * 2 + core, i * 2 + core))
    return lax.ppermute(shard, (axis, "core"), pairs)


def from_ahead(shard, axis):
    return turn(shard, axis, 1)


def from_behind(shard, axis):
    return turn(shard, axis, -1)


def cross(shard, axes, by):
    sizes = [lax.axis_size(axis) for axis in ("x", "y")]
    pairs = []
    for i in range(sizes[0]):
        for j in range(sizes[1]):
            for core in range(2):
                source = {"x": i, "y": j}
                source[axes[core]] = (source[axes[core]] + by) % sizes[0]
                pairs.append((((source["x"] * sizes[1]) + source["y"]) * 2 + core, (i * sizes[1] + j) * 2 + core))
    return lax.ppermute(shard, ("x", "y", "core"), pairs)


def swap(shard):
    return lax.ppermute(shard, "core", [(0, 1), (1, 0)])


def call(body, out, name, ins, scratch=(), cost=(0, 0), room=8, **extra):
    return pl.pallas_call(
        body,
        out_shape=out,
        scratch_shapes=list(scratch),
        name=name,
        cost_estimate=pl.CostEstimate(flops=cost[0], bytes_accessed=cost[1], transcendentals=0),
        compiler_params=pltpu.CompilerParams(vmem_limit_bytes=room * MIB),
        **extra,
    )(*ins)


def shape(*sizes, dtype=BF16):
    return jax.ShapeDtypeStruct(sizes, dtype)


def in_vmem(array):
    return pltpu.with_memory_space_constraint(array, pltpu.VMEM)


def in_hbm(array):
    return pltpu.with_memory_space_constraint(array, pltpu.MemorySpace.HBM)


def make_bands(filters, out):
    groups, count = filters.shape
    lag = lax.broadcasted_iota(jnp.int32, (count, 2 * count), 0)
    column = lax.broadcasted_iota(jnp.int32, (count, 2 * count), 1)
    turned = (lag + column == count).astype(BF16)
    base = jnp.dot(filters[...].astype(BF16), turned, preferred_element_type=F32)
    for g in range(groups):
        row = jnp.broadcast_to(base[g : g + 1, :], (count, 2 * count))
        out[g * count : (g + 1) * count, :] = pltpu.roll(
            row, 0, 1, stride=1, stride_axis=0
        ).astype(BF16)


def three_taps(work, taps, stream, rows):
    return (
        taps[0, stream : stream + 1, :] * work[8 : 8 + rows, :]
        + taps[1, stream : stream + 1, :] * work[7 : 7 + rows, :]
        + taps[2, stream : stream + 1, :] * work[6 : 6 + rows, :]
    )


def project_kernel(half, done, place, *refs):
    pieces, weight = refs[:8], refs[8]
    if half == 0:
        filters, short, bias = refs[9:12]
        total, bands, taps, direct = refs[12:16]
        rows, held, row_sems, weight_sems, small, small_sems = refs[16:]
    else:
        before, taps = refs[9:11]
        out, edge = refs[-8:-6]
        rows, held, row_sems, weight_sems, total, work = refs[-6:]
    slots, _, tile, _ = held.shape
    parts, _, span = rows.shape
    per_part = span // tile
    steps = parts * per_part
    sign = 1 - 2 * place[1]

    def bring(n, t):
        far = sign * (n // 2)
        z = lax.rem(place[0] + (far if n % 2 == 0 else -far) + 4, 4)
        core = place[1] if n % 2 == 0 else 1 - place[1]
        row = pl.ds(pl.multiple_of(z * 64 + core * 32, 32), 32)
        depth = pl.ds((done + t) * span, span)
        return pltpu.make_async_copy(pieces[n].at[:, depth], rows.at[t, row, :], row_sems.at[n, t])

    def fetch(k):
        depth = pl.ds(done * span + k * tile, tile)
        return pltpu.make_async_copy(
            weight.at[:, depth, :], held.at[k % slots], weight_sems.at[k % slots]
        )

    for n in range(8):
        bring(n, 0).start()
    for k in range(min(slots, steps)):
        fetch(k).start()
    if half == 0:
        little = [
            pltpu.make_async_copy(source, target, small_sems.at[n])
            for n, (source, target) in enumerate(((filters, small), (short, taps), (bias, direct)))
        ]
        for copy in little:
            copy.start()
    for t in range(1, parts):
        for n in range(8):
            bring(n, t).start()
    if half == 0:
        for copy in little:
            copy.wait()
        make_bands(small, bands)
        total[...] = jnp.zeros_like(total)
    else:
        total[...] = before[...]

    for t in range(parts):
        for n in range(8):
            bring(n, t).wait()
        for u in range(per_part):
            k = t * per_part + u
            fetch(k).wait()
            left = rows[t, :, u * tile : (u + 1) * tile]
            for s in range(3):
                total[:, s * 512 : (s + 1) * 512] += jnp.dot(
                    left, held[k % slots, s], preferred_element_type=F32
                )
            if k + slots < steps:
                fetch(k + slots).start()

    if half == 1:
        out[...] = total[...].astype(BF16)
        streams = []
        for s in (1, 2):
            work[...] = out[112:256, s * 512 : (s + 1) * 512].astype(F32)[8:, :]
            streams.append(three_taps(work, taps, s, 128))
        edge[0:128, :] = (streams[0] * streams[1]).astype(BF16)
        for s in range(3):
            edge[128 + 16 * s : 144 + 16 * s, :] = out[240:256, s * 512 : (s + 1) * 512]


def mix_kernel(projected, edge, taps, bias, bands, one, two, out, work, window, query):
    streams = []
    for s in range(3):
        work[0:8, :] = edge[128 + 16 * s : 144 + 16 * s, :].astype(F32)[8:16, :]
        work[8:264, :] = projected[:, s * 512 : (s + 1) * 512].astype(F32)
        featured = three_taps(work, taps, s, 256)
        if s == 0:
            query[...] = featured
        else:
            streams.append(featured)
    product = (streams[0] * streams[1]).astype(BF16)
    window[0:128, :] = edge[0:128, :]
    window[128:384, :] = product
    lane = lax.broadcasted_iota(jnp.int32, (128, 128), 1) // 16
    for j in range(4):
        columns = slice(j * 128, (j + 1) * 128)
        right = jnp.concatenate([window[0:256, columns], window[128:384, columns]], axis=1)
        result = jnp.dot(
            bands[j * 1024 : (j + 1) * 1024, :], right, preferred_element_type=F32
        )
        for block in range(2):
            filtered = jnp.zeros((128, 128), F32)
            for g in range(8):
                filtered = jnp.where(
                    lane == g,
                    result[g * 128 : (g + 1) * 128, block * 128 : (block + 1) * 128],
                    filtered,
                )
            rows = slice(block * 128, (block + 1) * 128)
            direct = window[128 + block * 128 : 256 + block * 128, columns].astype(F32)
            out[rows, columns] = (
                query[rows, columns] * (filtered + bias[:, columns] * direct)
            ).astype(BF16)


def out_kernel(count, blocks, place, gated, *refs):
    groups = refs[:count]
    keep, send, left, held, sems = refs[count:]
    copies = [
        pltpu.make_async_copy(groups[group].at[n], held.at[at], sems.at[at])
        for at, (_, group, n) in enumerate(blocks)
    ]
    for copy in copies:
        copy.start()
    for m in range(2):
        core = place[1] if m == 0 else 1 - place[1]
        sign = 1 - 2 * core
        for n, by in enumerate((0, 1, -1, 2)):
            z = lax.rem(place[0] + sign * by + 4, 4)
            row = pl.multiple_of(z * 64 + core * 32, 32)
            at = m * 128 + n * 32
            left[at : at + 32, :] = gated[pl.ds(row, 32), :]
    labels = [block[0] for block in blocks]
    for at, (near, far) in enumerate(labels):
        copies[at].wait()
        result = jnp.dot(left[...], held[at], preferred_element_type=F32).astype(BF16)
        to = labels.index((far, near))
        keep[:, at * 512 : (at + 1) * 512] = result[0:128]
        send[:, to * 512 : (to + 1) * 512] = result[128:256]


def pair_kernel(kept, got, *outs):
    for n, out in enumerate(outs):
        rows = slice(32 * n, 32 * (n + 1))
        out[...] = (kept[rows, :].astype(F32) + got[rows, :].astype(F32)).astype(BF16)


def join_kernel(a, b, out):
    out[...] = (a[...].astype(F32) + b[...].astype(F32)).astype(BF16)


def finish_kernel(plan, place, *refs):
    out = refs[-1]
    for h, labels in enumerate(plan):
        parts = refs[3 * h : 3 * h + 3]
        for n, (near, far) in enumerate(labels):
            x = lax.rem(place[2] + jnp.where(place[1] == 0, near, far) + 4, 4)
            y = lax.rem(place[3] + jnp.where(place[1] == 0, far, near) + 4, 4)
            column = pl.multiple_of((x * 4 + y) * 512, 512)
            at = slice(n * 512, (n + 1) * 512)
            total = parts[0][:, at].astype(F32)
            for part in parts[1:]:
                total += part[:, at].astype(F32)
            out[:, pl.ds(column, 512)] = total.astype(BF16)


def stack_kernel(count, *refs):
    sources, out, sems = refs[:count], refs[-2], refs[-1]
    copies = [
        pltpu.make_async_copy(source, out.at[n], sems.at[n]) for n, source in enumerate(sources)
    ]
    for copy in copies:
        copy.start()
    for copy in copies:
        copy.wait()


def stacked(arrays, after):
    count = len(arrays)
    return call(
        functools.partial(stack_kernel, count),
        shape(count, *arrays[0].shape),
        "stack",
        [*arrays, *after],
        [pltpu.SemaphoreType.DMA((count,))],
        (0, count * MIB),
        in_specs=[ANY] * (count + len(after)),
        out_specs=VM,
    )


def halves_kernel(ahead, behind, after, one, two, sems):
    copies = []
    for n, (source, target) in enumerate(
        ((ahead.at[0], one.at[0]), (ahead.at[1], one.at[1]), (behind.at[2], two.at[0]), (behind.at[3], two.at[1]))
    ):
        copies.append(pltpu.make_async_copy(source, target, sems.at[n]))
        copies[-1].start()
    for copy in copies:
        copy.wait()


NEAR, FAR = ("x", "y"), ("y", "x")


def spread(block, after):
    blocks = [block] + [cross(block, NEAR, by) for by in (1, -1, 2)]
    own = stacked([in_hbm(block)] + [in_vmem(block) for block in blocks[1:]], after)
    return [own] + [in_hbm(cross(own, FAR, by)) for by in (1, -1)]


def shards(tokens, in_weight, short_filter, mr_filter, mr_bias, out_weight):
    place = jnp.stack([lax.axis_index(a) for a in ("z", "core", "x", "y")]).astype(jnp.int32)

    pieces = []
    ahead = from_ahead(tokens, "z")
    for block in (tokens, ahead, from_ahead(ahead, "z"), from_behind(tokens, "z")):
        pieces += [block, swap(block)]
    pieces = [in_hbm(tokens)] + [in_vmem(piece) for piece in pieces[1:]]

    weights = spread(out_weight, [pieces[2], pieces[6]])

    weight = in_hbm(jnp.transpose(in_weight, (1, 0, 2)))
    span, slots, first = 1024, 5, 6

    def room(parts):
        return [
            pltpu.VMEM((parts, 256, span), BF16),
            pltpu.VMEM((slots, 3, 512, 512), BF16),
            pltpu.SemaphoreType.DMA((8, parts)),
            pltpu.SemaphoreType.DMA((slots,)),
        ]

    cost = (256 * 8192 * 1536, 14 * MIB)
    total, bands, taps, direct = call(
        functools.partial(project_kernel, 0, 0),
        (
            shape(256, 1536, dtype=F32),
            shape(4096, 256),
            shape(3, 3, 512, dtype=F32),
            shape(1, 512, dtype=F32),
        ),
        "project",
        [
            place,
            *pieces,
            weight,
            in_hbm(mr_filter.T),
            in_hbm(short_filter),
            in_hbm(mr_bias.reshape(1, 512)),
        ],
        room(first) + [pltpu.VMEM((32, 128), F32), pltpu.SemaphoreType.DMA((3,))],
        cost,
        16,
        in_specs=[SM] + [ANY] * 12,
        out_specs=(VM,) * 4,
    )
    relays = call(
        halves_kernel,
        (shape(2, 512, 512),) * 2,
        "halves",
        [*weights[1:], direct],
        [pltpu.SemaphoreType.DMA((4,))],
        (0, 4 * MIB),
        in_specs=[ANY] * 3,
        out_specs=(VM, VM),
    )
    weights += [cross(relays[0], FAR, 1), cross(relays[1], FAR, -1)]
    projected, edge = call(
        functools.partial(project_kernel, 1, first),
        (shape(256, 1536), shape(176, 512)),
        "project",
        [place, *pieces, weight, total, taps, relays[0]],
        room(8 - first) + [pltpu.VMEM((256, 1536), F32), pltpu.VMEM((136, 512), F32)],
        cost,
        18,
        in_specs=[SM] + [ANY] * 9 + [VM, VM, ANY],
        out_specs=(VM, VM),
    )

    context = ("x", "y")
    count = lax.axis_size(context)
    earlier = lax.ppermute(edge, context, [(i, i + 1) for i in range(count - 1)])
    gated = call(
        mix_kernel,
        shape(256, 512),
        "mix",
        [projected, earlier, taps, direct, bands, *weights[3:]],
        [pltpu.VMEM((264, 512), F32), pltpu.VMEM((384, 512), BF16), pltpu.VMEM((256, 512), F32)],
        (2 * 4096 * 256 * 256, 4 * MIB),
        in_specs=[VM] * 5 + [ANY] * 2,
        out_specs=VM,
    )

    steps = (0, 1, -1, 2)
    chunks = (
        (weights[:3], [((n, f), g, m) for g, f in enumerate(steps[:3]) for m, n in enumerate(steps[:3])]),
        (
            weights,
            [((2, f), g, 3) for g, f in enumerate(steps[:3])]
            + [((n, 2), 3 + m // 2, m % 2) for m, n in enumerate(steps)],
        ),
    )
    sums = []
    plan = []
    for groups, blocks in chunks:
        width = 512 * len(blocks)
        keep, send = call(
            functools.partial(out_kernel, len(groups), blocks),
            (shape(128, width),) * 2,
            "out",
            [place, gated, *groups],
            [
                pltpu.VMEM((256, 512), BF16),
                pltpu.VMEM((len(blocks), 512, 512), BF16),
                pltpu.SemaphoreType.DMA((len(blocks),)),
            ],
            (2 * 256 * 512 * width, 512 * width * 2),
            10,
            in_specs=[SM, VM] + [ANY] * len(groups),
            out_specs=(VM, VM),
        )
        here, front, back, across = call(
            pair_kernel,
            (shape(32, width),) * 4,
            "pair",
            [keep, swap(send)],
            cost=(0, 768 * width),
            in_specs=[VM, VM],
            out_specs=(VM,) * 4,
        )
        back = from_ahead(back, "z")
        joined = call(
            join_kernel,
            shape(32, width),
            "join",
            [front, from_behind(across, "z")],
            cost=(0, 192 * width),
            in_specs=[VM, VM],
            out_specs=VM,
        )
        parts = [here, back, from_behind(joined, "z")]
        sums += parts
        plan.append([block[0] for block in blocks])
    return call(
        functools.partial(finish_kernel, plan),
        shape(32, 8192),
        "finish",
        [place, *sums],
        cost=(0, 3 * MIB),
        in_specs=[SM] + [VM] * len(sums),
        out_specs=VM,
    )


def solution(mesh):
    grid = Mesh(mesh.devices.reshape(4, 4, 4, 2), ("x", "y", "z", "core"))
    channels = ("z", "core")
    context = ("x", "y")
    return jax.shard_map(
        shards,
        mesh=grid,
        in_specs=(
            P(context + channels, None),
            P(None, None, channels),
            P(None, None, channels),
            P(None, channels),
            P(channels),
            P(channels, context),
        ),
        out_specs=P(context + channels, None),
        check_vma=False,
    )
```
